32 devices in a mesh: energy: 8 (over y, x, core), slab: 4 (over z).
Axes of the slice: x: 2, y: 2, z: 4, core: 2. Of those that a mesh axis runs over, the one named last changes fastest.
Arguments:
- green: bfloat16 [8, 4, 2, 384, 384], P('energy', 'slab'), may hold values from -6 to 6
- weights: int32 [8, 2, 2], P('energy'), may hold values from 1 to 63
- coupling_m: bfloat16 [2, 384, 384], replicated, may hold values from -0.3125 to 0.3125
- coupling_n: bfloat16 [2, 384, 384], replicated, may hold values from -0.3125 to 0.3125
Outputs:
- sigma: bfloat16 [8, 4, 2, 384, 384], P('energy', 'slab')
The draws below stay inside these ranges and needn't reach their ends.
All inputs are finite; a program needn't handle non-finite values.
Results may differ from the reference program's by a relative error of at most 0.0061.
Values may be sent and summed in bfloat16 or wider, within the bound.
No kernel may reach another device: no remote copies, remote signals or barrier semaphores. Data moves between devices by JAX's collectives and lax.ppermute only.
A program may use at most 64 MiB of HBM per device.

```python
import jax
import jax.numpy as jnp
from jax import lax

B = 384
MODES = 2
K1 = 3
K2 = 7
NE = 8
NS = 4


def touch_ends(array, stream_key, smallest, largest):
    dims = array.shape
    spot = [jax.random.randint(jax.random.fold_in(stream_key, axis), (), 0, dims[axis]) for axis in range(len(dims))]
    array = array.at[tuple(spot)].set(smallest)
    longest = dims.index(max(dims))
    spot[longest] = (spot[longest] + 1) % dims[longest]
    return array.at[tuple(spot)].set(largest)


def levels(own_key, extent, split, least, high):
    def one(position, blocks):
        draws = jax.random.uniform(jax.random.fold_in(jax.random.fold_in(own_key, 6), position), (blocks,), jnp.float32, least / len(split), high / len(split))
        return jnp.repeat(jnp.exp(draws), extent[position] // blocks).reshape((-1,) + (1,) * (len(extent) - position - 1))

    gain = one(*split[0])
    for cut in split[1:]:
        gain = gain * one(*cut)
    return gain


def gaussian(key, shape, spread, limit, pieces=(), kind=jnp.bfloat16):
    level = levels(key, shape, pieces, -0.22, 0.18) if pieces else 1.0
    values = jax.random.normal(key, shape, jnp.float32) * spread * level
    return jnp.minimum(jnp.maximum(values, -limit), limit).astype(kind)


def setup_inputs(seed: int = 0) -> dict:
    key_list = jax.random.split(jax.random.key(seed), 5)
    return {
        "green": gaussian(key_list[0], (NE, NS, 2, B, B), 1.0, 6.0, ((0, 8), (1, 4))),
        "weights": touch_ends(jax.random.randint(key_list[1], (NE, MODES, 2), 1, 64), jax.random.fold_in(key_list[1], 1), 1, 63).astype(jnp.int32),
        "coupling_m": gaussian(key_list[2], (MODES, B, B), B ** -0.5, 0.3125),
        "coupling_n": gaussian(key_list[3], (MODES, B, B), B ** -0.5, 0.3125),
    }


def transform(mat, combo):
    left = jnp.einsum('ij,spjk->spik', mat.astype(jnp.float32), combo.astype(jnp.float32)).astype(jnp.bfloat16)
    return left, mat


def apply_right(left, mat):
    return jnp.einsum('spik,lk->spil', left.astype(jnp.float32), mat.astype(jnp.float32))


def reference(green, weights, coupling_m, coupling_n):
    shifts = (K1, K2)
    count = green.shape[0]

    def one_energy(index):
        own = jnp.zeros(green.shape[1:], jnp.float32)
        term = jnp.zeros(green.shape[1:], jnp.float32)
        for mode in range(MODES):
            step = shifts[mode]
            up_index = index + step
            down_index = index - step
            up_valid = (up_index < count).astype(jnp.float32)
            down_valid = (down_index >= 0).astype(jnp.float32)
            upper = lax.dynamic_index_in_dim(green, jnp.clip(up_index, 0, count - 1).astype(jnp.int32), 0, False).astype(jnp.float32)
            lower = lax.dynamic_index_in_dim(green, jnp.clip(down_index, 0, count - 1).astype(jnp.int32), 0, False).astype(jnp.float32)
            wrow = lax.dynamic_index_in_dim(weights, index.astype(jnp.int32), 0, False).astype(jnp.float32) / 32.0
            combo = (wrow[mode, 0] * up_valid * upper + wrow[mode, 1] * down_valid * lower).astype(jnp.bfloat16)
            left_m, mat_m = transform(coupling_m[mode], combo)
            left_n, mat_n = transform(coupling_n[mode], combo)
            own = own + apply_right(left_m, mat_m)
            term = term + apply_right(left_n, mat_n)
        term = term.astype(jnp.bfloat16).astype(jnp.float32)
        shifted = jnp.concatenate([term[1:], jnp.zeros_like(term[:1])], axis=0)
        return (own + shifted).astype(jnp.bfloat16)

    return lax.map(one_energy, jnp.arange(count, dtype=jnp.int32))
```

```python
import functools

import jax
import jax.numpy as jnp
from jax import lax
from jax.experimental import pallas as pl
from jax.experimental.pallas import tpu as pltpu
from jax.sharding import PartitionSpec as P

SHIFTS = (3, 7)
F32, BF16 = jnp.float32, jnp.bfloat16
NT = (((1,), (1,)), ((), ()))


def matchings(count):
    left = {}
    for target in range(count):
        for mode, shift in enumerate(SHIFTS):
            for side, source in enumerate((target + shift, target - shift)):
                if 0 <= source < count:
                    left[source, target] = (mode, side)
    rounds = []
    while left:
        options = {}
        for source, target in sorted(left):
            options.setdefault(source, []).append(target)
        taken = {}

        def place(source, seen):
            for target in options[source]:
                if target not in seen:
                    seen.add(target)
                    if target not in taken or place(taken[target], seen):
                        taken[target] = source
                        return True
            return False

        for source in sorted(options):
            place(source, set())
        rounds.append({t: (s,) + left.pop((s, t)) for t, s in sorted(taken.items())})
    return rounds


def lookup(table, index):
    value = jnp.int32(table[0])
    for start in range(len(table)):
        if start and table[start] != table[start - 1]:
            value = jnp.where(index >= start, jnp.int32(table[start]), value)
    return value


def factors(plan, count, weights_ref):
    me = lax.axis_index("energy")
    rows = []
    for mode in range(len(SHIFTS)):
        row = []
        for step in plan:
            codes = [0] * count
            for target, (_, which, side) in step.items():
                if which == mode:
                    codes[target] = side + 1
            code = lookup(codes, me)
            picked = jnp.where(code == 2, weights_ref[0, mode, 1], weights_ref[0, mode, 0])
            row.append(jnp.where(code > 0, picked, 0).astype(F32) / 32.0)
        rows.append(row)
    return rows


def sent_modes(plan, count):
    me = lax.axis_index("energy")
    out = []
    for step in plan:
        modes = [0] * count
        for source, mode, _ in step.values():
            modes[source] = mode
        out.append(lookup(modes, me))
    return out


def dot(a, b):
    return jnp.dot(a, b, preferred_element_type=F32)


def dot_t(a, b):
    return lax.dot_general(a, b, NT, preferred_element_type=F32)


VM = pl.BlockSpec(memory_space=pltpu.VMEM)
SM = pl.BlockSpec(memory_space=pltpu.SMEM)
ANY = pl.BlockSpec(memory_space=pl.ANY)


def call(body, ins, outs, flops, *args):
    return pl.pallas_call(
        body,
        out_shape=outs,
        in_specs=ins,
        out_specs=[VM] * len(outs),
        cost_estimate=pl.CostEstimate(flops=flops, bytes_accessed=1 << 20, transcendentals=0),
        compiler_params=pltpu.CompilerParams(vmem_limit_bytes=24 << 20),
    )(*args)


def body(count, slabs, plan, green, weights, coupling_m, coupling_n):
    size = green.shape[-1]
    block = pltpu.VMEM((size, size), BF16)
    wide = pltpu.VMEM((size, size), F32)
    rounds = len(plan)
    product = 2 * size**3

    def split(green_ref, real_ref, imag_ref, sems):
        copies = [
            pltpu.make_async_copy(green_ref.at[0, 0, part], out, sems.at[part])
            for part, out in enumerate((real_ref, imag_ref))
        ]
        for copy in copies:
            copy.start()
        for copy in copies:
            copy.wait()

    real, imag = pl.pallas_call(
        split,
        out_shape=[block, block],
        in_specs=[ANY],
        out_specs=[VM, VM],
        scratch_shapes=[pltpu.SemaphoreType.DMA((2,))],
    )(green)

    def along(x, step):
        return lax.ppermute(x, "energy", [(s, t) for t, (s, _, _) in step.items()])

    def from_next(x):
        return lax.ppermute(x, "slab", [(s, (s - 1) % slabs) for s in range(slabs)])

    near = [along(imag, step) for step in plan]
    behind = from_next(real)

    def first(real_ref, cm_ref, *outs):
        for mode, out in zip(sent_modes(plan, count), outs):
            mat = cm_ref[mode]
            out[...] = dot_t(dot(mat, real_ref[...]).astype(BF16), mat)

    partial = call(first, [VM, VM], [wide] * rounds, 2 * rounds * product, real, coupling_m)

    def terms(weights_ref, cm_ref, cn_ref, *refs):
        got, (term_ref, left_ref) = refs[:rounds], refs[rounds:]
        total = None
        for mode, row in enumerate(factors(plan, count, weights_ref)):
            combo = sum(f * ref[...].astype(F32) for f, ref in zip(row, got)).astype(BF16)
            left_ref[mode] = dot(cm_ref[mode], combo).astype(BF16)
            piece = dot_t(dot(cn_ref[mode], combo).astype(BF16), cn_ref[mode])
            total = piece if total is None else total + piece
        term_ref[...] = total.astype(BF16)

    modes = len(SHIFTS)
    term, left = call(
        terms,
        [SM, VM, VM] + [VM] * rounds,
        [block, pltpu.VMEM((modes, size, size), BF16)],
        3 * modes * product,
        weights,
        coupling_m,
        coupling_n,
        *near,
    )
    term_next = from_next(term)

    def second(behind_ref, cn_ref, *refs):
        here = jnp.where(lax.axis_index("slab") < slabs - 1, 1.0, 0.0).astype(F32)
        for mode, part, out in zip(sent_modes(plan, count), refs[:rounds], refs[rounds:]):
            mat = cn_ref[mode]
            piece = dot_t(dot(mat, behind_ref[...]).astype(BF16), mat)
            out[...] = (part[...] + here * piece).astype(BF16)

    whole = call(
        second, [VM, VM] + [VM] * rounds, [block] * rounds, 2 * rounds * product, behind, coupling_n, *partial
    )
    arrived = [along(x, step) for x, step in zip(whole, plan)]

    def own_sum(left_ref, cm_ref, out):
        out[...] = sum(dot_t(left_ref[m], cm_ref[m]) for m in range(modes))

    (own,) = call(own_sum, [VM, VM], [wide], modes * product, left, coupling_m)

    def finish(weights_ref, own_ref, term_ref, *refs):
        got, out = refs[:rounds], refs[rounds]
        rows = factors(plan, count, weights_ref)
        scale = [sum(row[r] for row in rows) for r in range(rounds)]
        out[0, 0, 0] = sum(f * ref[...].astype(F32) for f, ref in zip(scale, got)).astype(BF16)
        here = jnp.where(lax.axis_index("slab") < slabs - 1, 1.0, 0.0).astype(F32)
        out[0, 0, 1] = (own_ref[...] + here * term_ref[...].astype(F32)).astype(BF16)

    return pl.pallas_call(
        finish,
        out_shape=jax.ShapeDtypeStruct(green.shape, BF16),
        in_specs=[SM] + [VM] * (2 + rounds),
        out_specs=VM,
        compiler_params=pltpu.CompilerParams(vmem_limit_bytes=24 << 20),
    )(weights, own, term_next, *arrived)


def solution(mesh):
    count, slabs = mesh.shape["energy"], mesh.shape["slab"]
    placed = (P("energy", "slab", None, None, None), P("energy", None, None), P(), P())
    return jax.shard_map(
        functools.partial(body, count, slabs, matchings(count)),
        mesh=mesh,
        in_specs=placed,
        out_specs=P("energy", "slab", None, None, None),
        check_vma=False,
    )
```

```python
import functools

import jax
import jax.numpy as jnp
from jax import lax
from jax.experimental import pallas as pl
from jax.experimental.pallas import tpu as pltpu
from jax.sharding import PartitionSpec as P

SHIFTS = (3, 7)
LONG = 400
F32, BF16 = jnp.float32, jnp.bfloat16
NT = (((1,), (1,)), ((), ()))


def matchings(count):
    left = {}
    for target in range(count):
        for mode, shift in enumerate(SHIFTS):
            for side, source in enumerate((target + shift, target - shift)):
                if 0 <= source < count:
                    left[source, target] = (mode, side)
    rounds = []
    while left:
        options = {}
        for source, target in sorted(left):
            options.setdefault(source, []).append(target)
        taken = {}

        def place(source, seen):
            for target in options[source]:
                if target not in seen:
                    seen.add(target)
                    if target not in taken or place(taken[target], seen):
                        taken[target] = source
                        return True
            return False

        for source in sorted(options):
            place(source, set())
        rounds.append({t: (s,) + left.pop((s, t)) for t, s in sorted(taken.items())})
    return rounds


def lookup(table, index):
    value = jnp.int32(table[0])
    for start in range(len(table)):
        if start and table[start] != table[start - 1]:
            value = jnp.where(index >= start, jnp.int32(table[start]), value)
    return value


def routes(plan, count):
    out = []
    for step in plan:
        took, gave = [0] * count, [0] * count
        for target, (source, mode, side) in step.items():
            took[target] = 1 + mode * 2 + side
            gave[source] = mode
        out.append((took, gave))
    return out


def arriving(route):
    code = lookup(route[0], lax.axis_index("energy"))
    slot = jnp.maximum(code - 1, 0)
    return slot // 2, slot % 2, code > 0


def exchange(count, slabs, odd):
    pairs = []
    for e in range(count):
        for s in range(slabs):
            other = s + 1 if s % 2 == odd else s - 1
            if 0 <= other < slabs:
                pairs.append((e * slabs + s, e * slabs + other))
            elif e ^ 1 < count:
                pairs.append((e * slabs + s, (e ^ 1) * slabs + s))
    return pairs


def dot(a, b):
    return jnp.dot(a, b, preferred_element_type=F32)


def dot_t(a, b):
    return lax.dot_general(a, b, NT, preferred_element_type=F32)


def couple(mat, x):
    return dot_t(dot(mat, x).astype(BF16), mat)


VM = pl.BlockSpec(memory_space=pltpu.VMEM)
SM = pl.BlockSpec(memory_space=pltpu.SMEM)
ANY = pl.BlockSpec(memory_space=pl.ANY)


def call(kernel, ins, outs, products, size, *args, scratch=()):
    return pl.pallas_call(
        kernel,
        out_shape=outs,
        in_specs=ins,
        out_specs=[VM] * len(outs),
        scratch_shapes=scratch,
        cost_estimate=pl.CostEstimate(flops=2 * products * size**3, bytes_accessed=1 << 20, transcendentals=0),
        compiler_params=pltpu.CompilerParams(vmem_limit_bytes=24 << 20),
    )(*args)


def body(count, slabs, plan, green, weights, coupling_m, coupling_n):
    size = green.shape[-1]
    block = pltpu.VMEM((size, size), BF16)
    wide = pltpu.VMEM((size, size), F32)
    rounds = len(plan)
    route = routes(plan, count)

    def split(green_ref, real_ref, imag_ref, sems):
        copies = [
            pltpu.make_async_copy(green_ref.at[0, 0, part], out, sems.at[part])
            for part, out in enumerate((real_ref, imag_ref))
        ]
        for copy in copies:
            copy.start()
        for copy in copies:
            copy.wait()

    real, imag = pl.pallas_call(
        split,
        out_shape=[block, block],
        in_specs=[ANY],
        out_specs=[VM, VM],
        scratch_shapes=[pltpu.SemaphoreType.DMA((2,))],
    )(green)

    def along(x, step):
        return lax.ppermute(x, "energy", [(s, t) for t, (s, _, _) in step.items()])

    def from_next(x):
        return [lax.ppermute(x, ("energy", "slab"), exchange(count, slabs, odd)) for odd in range(2)]

    def sent_mode(r):
        return lookup(route[r][1], lax.axis_index("energy"))

    near = [along(imag, step) for step in plan]
    behind = from_next(real)

    def first(weights_ref, real_ref, cm_ref, factor_ref, *outs):
        for r, out in enumerate(outs):
            mode, side, present = arriving(route[r])
            factor = jnp.where(present, weights_ref[0, mode, side], 0).astype(F32) / 32.0
            factor_ref[r] = jnp.full((8, size), factor, F32)
            out[...] = couple(cm_ref[sent_mode(r)], real_ref[...])

    factors, *partial = call(
        first,
        [SM, VM, VM],
        [pltpu.VMEM((rounds, 8, size), F32)] + [wide] * rounds,
        2 * rounds,
        size,
        weights,
        real,
        coupling_m,
    )

    def scaled(ref, factor_ref, r):
        return factor_ref[r, 0:1, :] * ref[...].astype(F32)

    def term_first(factor_ref, cn_ref, got_ref, out_ref):
        mode, _, present = arriving(route[0])
        ahead = lax.axis_index("slab") > 0

        @pl.when(present & ahead)
        def _():
            out_ref[...] = couple(cn_ref[mode], scaled(got_ref, factor_ref, 0).astype(BF16))

        @pl.when(jnp.logical_not(present & ahead))
        def _():
            out_ref[...] = jnp.zeros_like(out_ref)

    (begun,) = call(term_first, [VM, VM, VM], [wide], 2, size, factors, coupling_n, near[0])

    def even_only(even_ref, after_ref, out_ref):
        @pl.when(lax.axis_index("slab") % 2 == 0)
        def _():
            out_ref[...] = even_ref[...]

    (held,) = call(even_only, [VM, ANY], [block], 2, size, behind[0], begun)

    def whole(rs, after):
        def kernel(held_ref, odd_ref, cn_ref, after_ref, *refs):
            parts, outs, next_ref = refs[: len(rs)], refs[len(rs) : -1], refs[-1]
            slab = lax.axis_index("slab")
            here = slab < slabs - 1
            for odd, ref in enumerate((held_ref, odd_ref)):

                @pl.when(here & (slab % 2 == odd))
                def _():
                    next_ref[...] = ref[...]

            for r, part, out in zip(rs, parts, outs):

                @pl.when(here)
                def _():
                    out[...] = (part[...] + couple(cn_ref[sent_mode(r)], next_ref[...])).astype(BF16)

                @pl.when(jnp.logical_not(here))
                def _():
                    out[...] = part[...].astype(BF16)

        return call(
            kernel,
            [VM, VM, VM, ANY] + [VM] * len(rs),
            [block] * len(rs),
            2 * len(rs),
            size,
            held,
            behind[1],
            coupling_n,
            after,
            *[partial[r] for r in rs],
            scratch=[block],
        )

    results = whole([0], begun)
    arrived = [along(results[0], plan[0])]

    def term_rest(factor_ref, cn_ref, after_ref, begun_ref, *refs):
        got, out_ref, total_ref = refs[:-2], refs[-2], refs[-1]
        total_ref[...] = begun_ref[...]
        for r, ref in enumerate(got, 1):
            mode, _, present = arriving(route[r])

            @pl.when(present & (lax.axis_index("slab") > 0))
            def _():
                total_ref[...] += couple(cn_ref[mode], scaled(ref, factor_ref, r).astype(BF16))

        out_ref[...] = total_ref[...].astype(BF16)

    (term,) = call(
        term_rest,
        [VM, VM, ANY, VM] + [VM] * (rounds - 1),
        [block],
        2 * rounds - 2,
        size,
        factors,
        coupling_n,
        results[0],
        begun,
        *near[1:],
        scratch=[wide],
    )
    term_next = from_next(term)
    if rounds > 1:
        results = results + whole(list(range(1, rounds)), term)
        arrived += [along(results[r], plan[r]) for r in range(1, rounds)]

    def own_sum(factor_ref, cm_ref, after_ref, *refs):
        got, out_ref = refs[:-1], refs[-1]
        out_ref[...] = jnp.zeros_like(out_ref)
        for r, ref in enumerate(got):
            mode, _, present = arriving(route[r])

            @pl.when(present)
            def _():
                out_ref[...] += couple(cm_ref[mode], scaled(ref, factor_ref, r).astype(BF16))

    (own,) = call(
        own_sum, [VM, VM, ANY] + [VM] * rounds, [wide], 2 * rounds, size, factors, coupling_m, results[-1], *near
    )

    def real_first(factor_ref, got_ref, out_ref):
        out_ref[...] = scaled(got_ref, factor_ref, 0)

    (real_sum,) = call(real_first, [VM, VM], [wide], LONG, size, factors, arrived[0])

    def imag_part(odd, source):
        def kernel(own_ref, term_ref, source_ref, out_ref):
            slab = lax.axis_index("slab")
            mine = slab % 2 == odd
            last = slab == slabs - 1

            @pl.when(mine & jnp.logical_not(last))
            def _():
                out_ref[...] = (own_ref[...] + term_ref[...].astype(F32)).astype(BF16)

            if odd:

                @pl.when(last)
                def _():
                    out_ref[...] = own_ref[...].astype(BF16)

                @pl.when(jnp.logical_not(mine | last))
                def _():
                    out_ref[...] = source_ref[...]

        return call(kernel, [VM, VM, VM if odd else ANY], [block], LONG, size, own, term_next[odd], source)[0]

    imag_sum = imag_part(1, imag_part(0, real_sum))

    def finish(factor_ref, imag_ref, real_ref, *refs):
        got, out_ref, held_ref, sems = refs[: rounds - 1], refs[-3], refs[-2], refs[-1]
        imag_copy = pltpu.make_async_copy(imag_ref, out_ref.at[0, 0, 1], sems.at[1])
        imag_copy.start()
        total = real_ref[...]
        for r, ref in enumerate(got, 1):
            total += scaled(ref, factor_ref, r)
        held_ref[...] = total.astype(BF16)
        real_copy = pltpu.make_async_copy(held_ref, out_ref.at[0, 0, 0], sems.at[0])
        real_copy.start()
        imag_copy.wait()
        real_copy.wait()

    return pl.pallas_call(
        finish,
        out_shape=jax.ShapeDtypeStruct(green.shape, BF16),
        in_specs=[VM] * (2 + rounds),
        out_specs=ANY,
        scratch_shapes=[block, pltpu.SemaphoreType.DMA((2,))],
        compiler_params=pltpu.CompilerParams(vmem_limit_bytes=24 << 20),
    )(factors, imag_sum, real_sum, *arrived[1:])


def solution(mesh):
    count, slabs = mesh.shape["energy"], mesh.shape["slab"]
    placed = (P("energy", "slab", None, None, None), P("energy", None, None), P(), P())
    return jax.shard_map(
        functools.partial(body, count, slabs, matchings(count)),
        mesh=mesh,
        in_specs=placed,
        out_specs=P("energy", "slab", None, None, None),
        check_vma=False,
    )
```

```python
import functools

import jax
import jax.numpy as jnp
from jax import lax
from jax.experimental import pallas as pl
from jax.experimental.pallas import tpu as pltpu
from jax.sharding import PartitionSpec as P

SHIFTS = (3, 7)
KINDS = (1, 0)
LONG = 400
F32, BF16 = jnp.float32, jnp.bfloat16
NT = (((1,), (1,)), ((), ()))


def matchings(count):
    left = {}
    for target in range(count):
        for mode, shift in enumerate(SHIFTS):
            for side, source in enumerate((target + shift, target - shift)):
                if 0 <= source < count:
                    left[source, target] = (mode, side)
    rounds = []
    while left:
        options = {}
        for source, target in sorted(left):
            options.setdefault(source, []).append(target)
        taken = {}

        def place(source, seen):
            for target in options[source]:
                if target not in seen:
                    seen.add(target)
                    if target not in taken or place(taken[target], seen):
                        taken[target] = source
                        return True
            return False

        for source in sorted(options):
            place(source, set())
        rounds.append({t: (s,) + left.pop((s, t)) for t, s in sorted(taken.items())})
    return rounds


def lookup(table, index):
    value = jnp.int32(table[0])
    for start in range(len(table)):
        if start and table[start] != table[start - 1]:
            value = jnp.where(index >= start, jnp.int32(table[start]), value)
    return value


def routes(plan, count):
    out = []
    for step in plan:
        took, gave = [0] * count, [0] * count
        for target, (source, mode, side) in step.items():
            took[target] = 1 + mode * 2 + side
            gave[source] = mode
        out.append((took, gave))
    return out


def arriving(route):
    code = lookup(route[0], lax.axis_index("energy"))
    slot = jnp.maximum(code - 1, 0)
    return slot // 2, slot % 2, code > 0


def descent(count, slabs, kind):
    pairs = []
    for e in range(count):
        if e ^ 1 >= count and e % 2 != kind:
            continue
        for s in range(slabs):
            to = s - 1 if e % 2 == kind else s + 1
            if 0 <= to < slabs:
                pairs.append((e * slabs + s, e * slabs + to))
            elif e ^ 1 < count:
                pairs.append((e * slabs + s, (e ^ 1) * slabs + s))
    return pairs


def dot(a, b):
    return jnp.dot(a, b, preferred_element_type=F32)


def dot_t(a, b):
    return lax.dot_general(a, b, NT, preferred_element_type=F32)


def couple(mat, x):
    return dot_t(dot(mat, x).astype(BF16), mat)


VM = pl.BlockSpec(memory_space=pltpu.VMEM)
SM = pl.BlockSpec(memory_space=pltpu.SMEM)
ANY = pl.BlockSpec(memory_space=pl.ANY)


def call(kernel, ins, outs, products, size, *args, scratch=()):
    return pl.pallas_call(
        kernel,
        out_shape=outs,
        in_specs=ins,
        out_specs=[VM] * len(outs),
        scratch_shapes=scratch,
        cost_estimate=pl.CostEstimate(flops=2 * products * size**3, bytes_accessed=1 << 20, transcendentals=0),
        compiler_params=pltpu.CompilerParams(vmem_limit_bytes=24 << 20),
    )(*args)


def body(count, slabs, plan, green, weights, coupling_m, coupling_n):
    size = green.shape[-1]
    block = pltpu.VMEM((size, size), BF16)
    wide = pltpu.VMEM((size, size), F32)
    rounds = len(plan)
    route = routes(plan, count)

    def split(green_ref, real_ref, imag_ref, sems):
        copies = [
            pltpu.make_async_copy(green_ref.at[0, 0, part], out, sems.at[part])
            for part, out in enumerate((real_ref, imag_ref))
        ]
        for copy in copies:
            copy.start()
        for copy in copies:
            copy.wait()

    real, imag = pl.pallas_call(
        split,
        out_shape=[block, block],
        in_specs=[ANY],
        out_specs=[VM, VM],
        scratch_shapes=[pltpu.SemaphoreType.DMA((2,))],
    )(green)

    def along(x, step):
        return lax.ppermute(x, "energy", [(s, t) for t, (s, _, _) in step.items()])

    def from_next(x):
        return [lax.ppermute(x, ("energy", "slab"), descent(count, slabs, kind)) for kind in KINDS]

    def sent_mode(r):
        return lookup(route[r][1], lax.axis_index("energy"))

    near = [along(imag, step) for step in plan]
    behind = from_next(real)

    def first(weights_ref, real_ref, cm_ref, factor_ref, *outs):
        for r, out in enumerate(outs):
            mode, side, present = arriving(route[r])
            factor = jnp.where(present, weights_ref[0, mode, side], 0).astype(F32) / 32.0
            factor_ref[r] = jnp.full((8, size), factor, F32)
            out[...] = couple(cm_ref[sent_mode(r)], real_ref[...])

    factors, *partial = call(
        first,
        [SM, VM, VM],
        [pltpu.VMEM((rounds, 8, size), F32)] + [wide] * rounds,
        2 * rounds,
        size,
        weights,
        real,
        coupling_m,
    )

    def scaled(ref, factor_ref, r):
        return factor_ref[r, 0:1, :] * ref[...].astype(F32)

    def term_first(factor_ref, cn_ref, got_ref, out_ref):
        mode, _, present = arriving(route[0])
        ahead = lax.axis_index("slab") > 0

        @pl.when(present & ahead)
        def _():
            out_ref[...] = couple(cn_ref[mode], scaled(got_ref, factor_ref, 0).astype(BF16))

        @pl.when(jnp.logical_not(present & ahead))
        def _():
            out_ref[...] = jnp.zeros_like(out_ref)

    (begun,) = call(term_first, [VM, VM, VM], [wide], 2, size, factors, coupling_n, near[0])

    def is_kind(k):
        return lax.axis_index("energy") % 2 == KINDS[k]

    def hold(one_ref, after_ref, out_ref):
        @pl.when(is_kind(0))
        def _():
            out_ref[...] = one_ref[...]

    (held,) = call(hold, [VM, ANY], [block], 2, size, behind[0], begun)

    def whole(rs, after):
        def kernel(held_ref, two_ref, cn_ref, after_ref, *refs):
            parts, outs, next_ref = refs[: len(rs)], refs[len(rs) : -1], refs[-1]
            here = lax.axis_index("slab") < slabs - 1
            for k, ref in enumerate((held_ref, two_ref)):

                @pl.when(here & is_kind(k))
                def _():
                    next_ref[...] = ref[...]

            for r, part, out in zip(rs, parts, outs):

                @pl.when(here)
                def _():
                    out[...] = (part[...] + couple(cn_ref[sent_mode(r)], next_ref[...])).astype(BF16)

                @pl.when(jnp.logical_not(here))
                def _():
                    out[...] = part[...].astype(BF16)

        return call(
            kernel,
            [VM, VM, VM, ANY] + [VM] * len(rs),
            [block] * len(rs),
            2 * len(rs),
            size,
            held,
            behind[1],
            coupling_n,
            after,
            *[partial[r] for r in rs],
            scratch=[block],
        )

    results = whole([0], begun)
    arrived = [along(results[0], plan[0])]

    def term_rest(factor_ref, cn_ref, after_ref, begun_ref, *refs):
        got, out_ref, total_ref = refs[:-2], refs[-2], refs[-1]
        total_ref[...] = begun_ref[...]
        for r, ref in enumerate(got, 1):
            mode, _, present = arriving(route[r])

            @pl.when(present & (lax.axis_index("slab") > 0))
            def _():
                total_ref[...] += couple(cn_ref[mode], scaled(ref, factor_ref, r).astype(BF16))

        out_ref[...] = total_ref[...].astype(BF16)

    (term,) = call(
        term_rest,
        [VM, VM, ANY, VM] + [VM] * (rounds - 1),
        [block],
        2 * rounds - 2,
        size,
        factors,
        coupling_n,
        results[0],
        begun,
        *near[1:],
        scratch=[wide],
    )
    term_next = from_next(term)
    if rounds > 1:
        results = results + whole(list(range(1, rounds)), term)
        arrived += [along(results[r], plan[r]) for r in range(1, rounds)]

    def own_sum(factor_ref, cm_ref, after_ref, *refs):
        got, out_ref = refs[:-1], refs[-1]
        out_ref[...] = jnp.zeros_like(out_ref)
        for r, ref in enumerate(got):
            mode, _, present = arriving(route[r])

            @pl.when(present)
            def _():
                out_ref[...] += couple(cm_ref[mode], scaled(ref, factor_ref, r).astype(BF16))

    (own,) = call(
        own_sum, [VM, VM, ANY] + [VM] * rounds, [wide], 2 * rounds, size, factors, coupling_m, results[-1], *near
    )

    def real_first(factor_ref, got_ref, out_ref):
        out_ref[...] = scaled(got_ref, factor_ref, 0)

    (real_sum,) = call(real_first, [VM, VM], [wide], LONG, size, factors, arrived[0])

    def imag_part(k, source):
        def kernel(own_ref, term_ref, source_ref, out_ref):
            last = lax.axis_index("slab") == slabs - 1

            @pl.when(is_kind(k) & jnp.logical_not(last))
            def _():
                out_ref[...] = (own_ref[...] + term_ref[...].astype(F32)).astype(BF16)

            @pl.when(is_kind(k) & last)
            def _():
                out_ref[...] = own_ref[...].astype(BF16)

            if k:

                @pl.when(is_kind(0))
                def _():
                    out_ref[...] = source_ref[...]

        return call(kernel, [VM, VM, VM if k else ANY], [block], LONG, size, own, term_next[k], source)[0]

    imag_sum = imag_part(1, imag_part(0, real_sum))

    def finish(factor_ref, imag_ref, real_ref, *refs):
        got, out_ref, held_ref, sems = refs[: rounds - 1], refs[-3], refs[-2], refs[-1]
        imag_copy = pltpu.make_async_copy(imag_ref, out_ref.at[0, 0, 1], sems.at[1])
        imag_copy.start()
        total = real_ref[...]
        for r, ref in enumerate(got, 1):
            total += scaled(ref, factor_ref, r)
        held_ref[...] = total.astype(BF16)
        real_copy = pltpu.make_async_copy(held_ref, out_ref.at[0, 0, 0], sems.at[0])
        real_copy.start()
        imag_copy.wait()
        real_copy.wait()

    return pl.pallas_call(
        finish,
        out_shape=jax.ShapeDtypeStruct(green.shape, BF16),
        in_specs=[VM] * (2 + rounds),
        out_specs=ANY,
        scratch_shapes=[block, pltpu.SemaphoreType.DMA((2,))],
        compiler_params=pltpu.CompilerParams(vmem_limit_bytes=24 << 20),
    )(factors, imag_sum, real_sum, *arrived[1:])


def solution(mesh):
    count, slabs = mesh.shape["energy"], mesh.shape["slab"]
    placed = (P("energy", "slab", None, None, None), P("energy", None, None), P(), P())
    return jax.shard_map(
        functools.partial(body, count, slabs, matchings(count)),
        mesh=mesh,
        in_specs=placed,
        out_specs=P("energy", "slab", None, None, None),
        check_vma=False,
    )
```

```python
import functools

import jax
import jax.numpy as jnp
from jax import lax
from jax.experimental import pallas as pl
from jax.experimental.pallas import tpu as pltpu
from jax.sharding import PartitionSpec as P

SHIFTS = (3, 7)
KINDS = (1, 0)
LONG = 400
SHORT = 2
F32, BF16 = jnp.float32, jnp.bfloat16
NT = (((1,), (1,)), ((), ()))


def matchings(count):
    left = {}
    for target in range(count):
        for mode, shift in enumerate(SHIFTS):
            for side, source in enumerate((target + shift, target - shift)):
                if 0 <= source < count:
                    left[source, target] = (mode, side)
    rounds = []
    while left:
        options = {}
        for source, target in sorted(left):
            options.setdefault(source, []).append(target)
        taken = {}

        def place(source, seen):
            for target in options[source]:
                if target not in seen:
                    seen.add(target)
                    if target not in taken or place(taken[target], seen):
                        taken[target] = source
                        return True
            return False

        for source in sorted(options):
            place(source, set())
        rounds.append({t: (s,) + left.pop((s, t)) for t, s in sorted(taken.items())})
    return rounds


def lookup(table, index):
    value = jnp.int32(table[0])
    for start in range(len(table)):
        if start and table[start] != table[start - 1]:
            value = jnp.where(index >= start, jnp.int32(table[start]), value)
    return value


def routes(plan, count):
    out = []
    for step in plan:
        took, gave = [0] * count, [0] * count
        for target, (source, mode, side) in step.items():
            took[target] = 1 + mode * 2 + side
            gave[source] = mode
        out.append((took, gave))
    return out


def arriving(route):
    code = lookup(route[0], lax.axis_index("energy"))
    slot = jnp.maximum(code - 1, 0)
    return slot // 2, slot % 2, code > 0


def descent(count, slabs, kind):
    pairs = []
    for e in range(count):
        if e ^ 1 >= count and e % 2 != kind:
            continue
        for s in range(slabs):
            to = s - 1 if e % 2 == kind else s + 1
            if 0 <= to < slabs:
                pairs.append((e * slabs + s, e * slabs + to))
            elif e ^ 1 < count:
                pairs.append((e * slabs + s, (e ^ 1) * slabs + s))
    return pairs


def closed(step, count):
    sources = {source for source, _, _ in step.values()}
    return count % 2 == 0 and sources == set(step) and all((e in step) != (e + 1 in step) for e in range(0, count, 2))


def dot(a, b):
    return jnp.dot(a, b, preferred_element_type=F32)


def dot_t(a, b):
    return lax.dot_general(a, b, NT, preferred_element_type=F32)


def couple(mat, x):
    return dot_t(dot(mat, x).astype(BF16), mat)


VM = pl.BlockSpec(memory_space=pltpu.VMEM)
SM = pl.BlockSpec(memory_space=pltpu.SMEM)
ANY = pl.BlockSpec(memory_space=pl.ANY)


def call(kernel, ins, outs, products, size, *args, scratch=()):
    return pl.pallas_call(
        kernel,
        out_shape=outs,
        in_specs=ins,
        out_specs=[VM] * len(outs),
        scratch_shapes=scratch,
        cost_estimate=pl.CostEstimate(flops=2 * products * size**3, bytes_accessed=1 << 20, transcendentals=0),
        compiler_params=pltpu.CompilerParams(vmem_limit_bytes=24 << 20),
    )(*args)


def body(count, slabs, plan, green, weights, coupling_m, coupling_n):
    size = green.shape[-1]
    block = pltpu.VMEM((size, size), BF16)
    wide = pltpu.VMEM((size, size), F32)
    rounds = len(plan)
    route = routes(plan, count)

    def split(green_ref, real_ref, imag_ref, sems):
        copies = [
            pltpu.make_async_copy(green_ref.at[0, 0, part], out, sems.at[part])
            for part, out in enumerate((real_ref, imag_ref))
        ]
        for copy in copies:
            copy.start()
        for copy in copies:
            copy.wait()

    real, imag = pl.pallas_call(
        split,
        out_shape=[block, block],
        in_specs=[ANY],
        out_specs=[VM, VM],
        scratch_shapes=[pltpu.SemaphoreType.DMA((2,))],
    )(green)

    def along(x, step):
        return lax.ppermute(x, "energy", [(s, t) for t, (s, _, _) in step.items()])

    def along_closed(x, step):
        if not closed(step, count):
            return along(x, step)
        swapped = lax.ppermute(x, "energy", [(e, e ^ 1) for e in range(count)])
        pairs = [(s ^ 1, t) for t, (s, _, _) in step.items()] + [(t, t ^ 1) for t in step]
        return lax.ppermute(swapped, "energy", pairs)

    def from_next(x):
        return [lax.ppermute(x, ("energy", "slab"), descent(count, slabs, kind)) for kind in KINDS]

    def sent_mode(r):
        return lookup(route[r][1], lax.axis_index("energy"))

    near = [along(imag, step) for step in plan]
    behind = from_next(real)

    def first(weights_ref, real_ref, cm_ref, factor_ref, *outs):
        for r, out in enumerate(outs):
            mode, side, present = arriving(route[r])
            factor = jnp.where(present, weights_ref[0, mode, side], 0).astype(F32) / 32.0
            factor_ref[r] = jnp.full((8, size), factor, F32)
            out[...] = couple(cm_ref[sent_mode(r)], real_ref[...])

    factors, *partial = call(
        first,
        [SM, VM, VM],
        [pltpu.VMEM((rounds, 8, size), F32)] + [wide] * rounds,
        2 * rounds,
        size,
        weights,
        real,
        coupling_m,
    )

    def scaled(ref, factor_ref, r):
        return factor_ref[r, 0:1, :] * ref[...].astype(F32)

    def is_kind(k):
        return lax.axis_index("energy") % 2 == KINDS[k]

    def hold(one_ref, after_ref, out_ref):
        @pl.when(is_kind(0))
        def _():
            out_ref[...] = one_ref[...]

    (held,) = call(hold, [VM, ANY], [block], 2, size, behind[0], factors)

    def whole(rs, after):
        def kernel(held_ref, two_ref, cn_ref, after_ref, *refs):
            parts, outs, next_ref = refs[: len(rs)], refs[len(rs) : -1], refs[-1]
            here = lax.axis_index("slab") < slabs - 1
            for k, ref in enumerate((held_ref, two_ref)):

                @pl.when(here & is_kind(k))
                def _():
                    next_ref[...] = ref[...]

            for r, part, out in zip(rs, parts, outs):

                @pl.when(here)
                def _():
                    out[...] = (part[...] + couple(cn_ref[sent_mode(r)], next_ref[...])).astype(BF16)

                @pl.when(jnp.logical_not(here))
                def _():
                    out[...] = part[...].astype(BF16)

        return call(
            kernel,
            [VM, VM, VM, ANY] + [VM] * len(rs),
            [block] * len(rs),
            2 * len(rs),
            size,
            held,
            behind[1],
            coupling_n,
            after,
            *[partial[r] for r in rs],
            scratch=[block],
        )

    results = whole([0], factors)
    arrived = [along(results[0], plan[0])]
    if rounds > 1:
        results = results + whole(list(range(1, rounds)), results[0])
        arrived += [along_closed(results[r], plan[r]) for r in range(1, rounds)]

    def term_first(factor_ref, cn_ref, got_ref, after_ref, out_ref):
        mode, _, present = arriving(route[0])
        ahead = lax.axis_index("slab") > 0

        @pl.when(present & ahead)
        def _():
            out_ref[...] = couple(cn_ref[mode], scaled(got_ref, factor_ref, 0).astype(BF16))

        @pl.when(jnp.logical_not(present & ahead))
        def _():
            out_ref[...] = jnp.zeros_like(out_ref)

    (begun,) = call(term_first, [VM, VM, VM, ANY], [wide], 2, size, factors, coupling_n, near[0], results[-1])

    def term_rest(factor_ref, cn_ref, after_ref, begun_ref, *refs):
        got, out_ref, total_ref = refs[:-2], refs[-2], refs[-1]
        total_ref[...] = begun_ref[...]
        for r, ref in enumerate(got, 1):
            mode, _, present = arriving(route[r])

            @pl.when(present & (lax.axis_index("slab") > 0))
            def _():
                total_ref[...] += couple(cn_ref[mode], scaled(ref, factor_ref, r).astype(BF16))

        out_ref[...] = total_ref[...].astype(BF16)

    (term,) = call(
        term_rest,
        [VM, VM, ANY, VM] + [VM] * (rounds - 1),
        [block],
        LONG,
        size,
        factors,
        coupling_n,
        results[-1],
        begun,
        *near[1:],
        scratch=[wide],
    )
    term_next = from_next(term)

    def own_sum(factor_ref, cm_ref, after_ref, *refs):
        got, out_ref = refs[:-1], refs[-1]
        out_ref[...] = jnp.zeros_like(out_ref)
        for r, ref in enumerate(got):
            mode, _, present = arriving(route[r])

            @pl.when(present)
            def _():
                out_ref[...] += couple(cm_ref[mode], scaled(ref, factor_ref, r).astype(BF16))

    (own,) = call(
        own_sum, [VM, VM, ANY] + [VM] * rounds, [wide], 2 * rounds, size, factors, coupling_m, term, *near
    )

    def real_first(factor_ref, got_ref, out_ref):
        out_ref[...] = scaled(got_ref, factor_ref, 0)

    (real_sum,) = call(real_first, [VM, VM], [wide], SHORT, size, factors, arrived[0])

    def imag_part(k, source):
        def kernel(own_ref, term_ref, source_ref, out_ref):
            last = lax.axis_index("slab") == slabs - 1

            @pl.when(is_kind(k) & jnp.logical_not(last))
            def _():
                out_ref[...] = (own_ref[...] + term_ref[...].astype(F32)).astype(BF16)

            @pl.when(is_kind(k) & last)
            def _():
                out_ref[...] = own_ref[...].astype(BF16)

            if k:

                @pl.when(is_kind(0))
                def _():
                    out_ref[...] = source_ref[...]

        return call(kernel, [VM, VM, VM if k else ANY], [block], SHORT, size, own, term_next[k], source)[0]

    imag_sum = imag_part(1, imag_part(0, real_sum))

    def finish(factor_ref, imag_ref, real_ref, *refs):
        got, out_ref, held_ref, sems = refs[: rounds - 1], refs[-3], refs[-2], refs[-1]
        imag_copy = pltpu.make_async_copy(imag_ref, out_ref.at[0, 0, 1], sems.at[1])
        imag_copy.start()
        total = real_ref[...]
        for r, ref in enumerate(got, 1):
            total += scaled(ref, factor_ref, r)
        held_ref[...] = total.astype(BF16)
        real_copy = pltpu.make_async_copy(held_ref, out_ref.at[0, 0, 0], sems.at[0])
        real_copy.start()
        imag_copy.wait()
        real_copy.wait()

    return pl.pallas_call(
        finish,
        out_shape=jax.ShapeDtypeStruct(green.shape, BF16),
        in_specs=[VM] * (2 + rounds),
        out_specs=ANY,
        scratch_shapes=[block, pltpu.SemaphoreType.DMA((2,))],
        compiler_params=pltpu.CompilerParams(vmem_limit_bytes=24 << 20),
    )(factors, imag_sum, real_sum, *arrived[1:])


def solution(mesh):
    count, slabs = mesh.shape["energy"], mesh.shape["slab"]
    placed = (P("energy", "slab", None, None, None), P("energy", None, None), P(), P())
    return jax.shard_map(
        functools.partial(body, count, slabs, matchings(count)),
        mesh=mesh,
        in_specs=placed,
        out_specs=P("energy", "slab", None, None, None),
        check_vma=False,
    )
```

```python
import functools

import jax
import jax.numpy as jnp
from jax import lax
from jax.experimental import pallas as pl
from jax.experimental.pallas import tpu as pltpu
from jax.sharding import PartitionSpec as P

SHIFTS = (3, 7)
KINDS = (1, 0)
LONG = 400
SHORT = 2
F32, BF16 = jnp.float32, jnp.bfloat16
NT = (((1,), (1,)), ((), ()))


def matchings(count):
    left = {}
    for target in range(count):
        for mode, shift in enumerate(SHIFTS):
            for side, source in enumerate((target + shift, target - shift)):
                if 0 <= source < count:
                    left[source, target] = (mode, side)
    rounds = []
    while left:
        options = {}
        for source, target in sorted(left):
            options.setdefault(source, []).append(target)
        taken = {}

        def place(source, seen):
            for target in options[source]:
                if target not in seen:
                    seen.add(target)
                    if target not in taken or place(taken[target], seen):
                        taken[target] = source
                        return True
            return False

        for source in sorted(options):
            place(source, set())
        rounds.append({t: (s,) + left.pop((s, t)) for t, s in sorted(taken.items())})
    return rounds


def lookup(table, index):
    value = jnp.int32(table[0])
    for start in range(len(table)):
        if start and table[start] != table[start - 1]:
            value = jnp.where(index >= start, jnp.int32(table[start]), value)
    return value


def routes(plan, count):
    out = []
    for step in plan:
        took, gave = [0] * count, [0] * count
        for target, (source, mode, side) in step.items():
            took[target] = 1 + mode * 2 + side
            gave[source] = mode
        out.append((took, gave))
    return out


def arriving(route):
    code = lookup(route[0], lax.axis_index("energy"))
    slot = jnp.maximum(code - 1, 0)
    return slot // 2, slot % 2, code > 0


def descent(count, slabs, kind):
    pairs = []
    for e in range(count):
        if e ^ 1 >= count and e % 2 != kind:
            continue
        for s in range(slabs):
            to = s - 1 if e % 2 == kind else s + 1
            if 0 <= to < slabs:
                pairs.append((e * slabs + s, e * slabs + to))
            elif e ^ 1 < count:
                pairs.append((e * slabs + s, (e ^ 1) * slabs + s))
    return pairs


def closed(step, count):
    sources = {source for source, _, _ in step.values()}
    return count % 2 == 0 and sources == set(step) and all((e in step) != (e + 1 in step) for e in range(0, count, 2))


def dot(a, b):
    return jnp.dot(a, b, preferred_element_type=F32)


def dot_t(a, b):
    return lax.dot_general(a, b, NT, preferred_element_type=F32)


def couple(mat, x):
    return dot_t(dot(mat, x).astype(BF16), mat)


VM = pl.BlockSpec(memory_space=pltpu.VMEM)
SM = pl.BlockSpec(memory_space=pltpu.SMEM)
ANY = pl.BlockSpec(memory_space=pl.ANY)


def call(kernel, ins, outs, products, size, *args, scratch=()):
    return pl.pallas_call(
        kernel,
        out_shape=outs,
        in_specs=ins,
        out_specs=[VM] * len(outs),
        scratch_shapes=scratch,
        cost_estimate=pl.CostEstimate(flops=2 * products * size**3, bytes_accessed=1 << 20, transcendentals=0),
        compiler_params=pltpu.CompilerParams(vmem_limit_bytes=24 << 20),
    )(*args)


def body(count, slabs, plan, green, weights, coupling_m, coupling_n):
    size = green.shape[-1]
    block = pltpu.VMEM((size, size), BF16)
    wide = pltpu.VMEM((size, size), F32)
    rounds = len(plan)
    route = routes(plan, count)

    def split(green_ref, real_ref, imag_ref, sems):
        copies = [
            pltpu.make_async_copy(green_ref.at[0, 0, part], out, sems.at[part])
            for part, out in enumerate((real_ref, imag_ref))
        ]
        for copy in copies:
            copy.start()
        for copy in copies:
            copy.wait()

    real, imag = pl.pallas_call(
        split,
        out_shape=[block, block],
        in_specs=[ANY],
        out_specs=[VM, VM],
        scratch_shapes=[pltpu.SemaphoreType.DMA((2,))],
    )(green)

    def along(x, step):
        return lax.ppermute(x, "energy", [(s, t) for t, (s, _, _) in step.items()])

    def along_closed(x, step):
        if not closed(step, count):
            return along(x, step)
        swapped = lax.ppermute(x, "energy", [(e, e ^ 1) for e in range(count)])
        pairs = [(s ^ 1, t) for t, (s, _, _) in step.items()] + [(t, t ^ 1) for t in step]
        return lax.ppermute(swapped, "energy", pairs)

    def from_next(x):
        return [lax.ppermute(x, ("energy", "slab"), descent(count, slabs, kind)) for kind in KINDS]

    def sent_mode(r):
        return lookup(route[r][1], lax.axis_index("energy"))

    near = [along(imag, step) for step in plan]
    behind = from_next(real)

    def first(weights_ref, real_ref, cm_ref, cn_ref, factor_ref, near_ref, *rest):
        outs, sem = rest[:-1], rest[-1]
        copy = pltpu.make_async_copy(cn_ref, near_ref, sem)
        copy.start()
        for r, out in enumerate(outs):
            mode, side, present = arriving(route[r])
            factor = jnp.where(present, weights_ref[0, mode, side], 0).astype(F32) / 32.0
            factor_ref[r] = jnp.full((8, size), factor, F32)
            out[...] = couple(cm_ref[sent_mode(r)], real_ref[...])
        copy.wait()

    factors, coupling_n, *partial = call(
        first,
        [SM, VM, VM, ANY],
        [pltpu.VMEM((rounds, 8, size), F32), pltpu.VMEM(coupling_n.shape, BF16)] + [wide] * rounds,
        2 * rounds,
        size,
        weights,
        real,
        coupling_m,
        pltpu.with_memory_space_constraint(coupling_n, pltpu.HBM),
        scratch=[pltpu.SemaphoreType.DMA],
    )

    def scaled(ref, factor_ref, r):
        return factor_ref[r, 0:1, :] * ref[...].astype(F32)

    def is_kind(k):
        return lax.axis_index("energy") % 2 == KINDS[k]

    def own_result(r):
        sources = {source: mode for source, mode, _ in plan[r].values()}
        return lookup([int(e in sources and sources[e] != route[0][1][e]) for e in range(count)], lax.axis_index("energy"))

    def result(r, partial_ref, behind_ref, cn_ref, out_ref):
        here = lax.axis_index("slab") < slabs - 1

        @pl.when(here)
        def _():
            out_ref[...] = (partial_ref[...] + couple(cn_ref[sent_mode(r)], behind_ref[...])).astype(BF16)

        @pl.when(jnp.logical_not(here))
        def _():
            out_ref[...] = partial_ref[...].astype(BF16)

    def later_result(r, partial_ref, behind_ref, cn_ref, first_ref, out_ref):
        again = own_result(r) == 0

        @pl.when(again)
        def _():
            out_ref[...] = first_ref[...]

        @pl.when(jnp.logical_not(again))
        def _():
            result(r, partial_ref, behind_ref, cn_ref, out_ref)

    def early(behind_ref, cn_ref, *refs):
        parts, outs = refs[:rounds], refs[rounds:]

        @pl.when(is_kind(0))
        def _():
            result(0, parts[0], behind_ref, cn_ref, outs[0])
            for r in range(1, rounds):
                later_result(r, parts[r], behind_ref, cn_ref, outs[0], outs[r])

    ready = call(early, [VM] * (2 + rounds), [block] * rounds, 2, size, behind[0], coupling_n, *partial)

    def late(behind_ref, cn_ref, partial_ref, ready_ref, out_ref):
        @pl.when(is_kind(0))
        def _():
            out_ref[...] = ready_ref[...]

        @pl.when(is_kind(1))
        def _():
            result(0, partial_ref, behind_ref, cn_ref, out_ref)

    results = call(late, [VM] * 4, [block], 2, size, behind[1], coupling_n, partial[0], ready[0])
    arrived = [along(results[0], plan[0])]

    def late_rest(behind_ref, cn_ref, first_ref, *refs):
        for r in range(1, rounds):
            part, done, out = (refs[r - 1 + k * (rounds - 1)] for k in range(3))

            @pl.when(is_kind(0))
            def _():
                out[...] = done[...]

            @pl.when(is_kind(1))
            def _():
                later_result(r, part, behind_ref, cn_ref, first_ref, out)

    if rounds > 1:
        results = list(results) + list(
            call(
                late_rest,
                [VM] * (3 + 2 * (rounds - 1)),
                [block] * (rounds - 1),
                2,
                size,
                behind[1],
                coupling_n,
                results[0],
                *partial[1:],
                *ready[1:],
            )
        )
        arrived += [along_closed(results[r], plan[r]) for r in range(1, rounds)]

    def term_first(factor_ref, cn_ref, got_ref, after_ref, out_ref):
        mode, _, present = arriving(route[0])
        ahead = lax.axis_index("slab") > 0

        @pl.when(present & ahead)
        def _():
            out_ref[...] = couple(cn_ref[mode], scaled(got_ref, factor_ref, 0).astype(BF16))

        @pl.when(jnp.logical_not(present & ahead))
        def _():
            out_ref[...] = jnp.zeros_like(out_ref)

    (begun,) = call(term_first, [VM, VM, VM, ANY], [wide], 2, size, factors, coupling_n, near[0], results[-1])

    def term_rest(factor_ref, cn_ref, after_ref, begun_ref, *refs):
        got, out_ref, total_ref = refs[:-2], refs[-2], refs[-1]
        total_ref[...] = begun_ref[...]
        for r, ref in enumerate(got, 1):
            mode, _, present = arriving(route[r])

            @pl.when(present & (lax.axis_index("slab") > 0))
            def _():
                total_ref[...] += couple(cn_ref[mode], scaled(ref, factor_ref, r).astype(BF16))

        out_ref[...] = total_ref[...].astype(BF16)

    (term,) = call(
        term_rest,
        [VM, VM, ANY, VM] + [VM] * (rounds - 1),
        [block],
        LONG,
        size,
        factors,
        coupling_n,
        results[-1],
        begun,
        *near[1:],
        scratch=[wide],
    )
    term_next = from_next(term)

    def own_sum(factor_ref, cm_ref, after_ref, *refs):
        got, out_ref = refs[:-1], refs[-1]
        out_ref[...] = jnp.zeros_like(out_ref)
        for r, ref in enumerate(got):
            mode, _, present = arriving(route[r])

            @pl.when(present)
            def _():
                out_ref[...] += couple(cm_ref[mode], scaled(ref, factor_ref, r).astype(BF16))

    (own,) = call(
        own_sum, [VM, VM, ANY] + [VM] * rounds, [wide], 2 * rounds, size, factors, coupling_m, term, *near
    )

    def real_first(factor_ref, got_ref, out_ref):
        out_ref[...] = scaled(got_ref, factor_ref, 0)

    (real_sum,) = call(real_first, [VM, VM], [wide], SHORT, size, factors, arrived[0])

    def imag_part(k, source):
        def kernel(own_ref, term_ref, source_ref, out_ref):
            last = lax.axis_index("slab") == slabs - 1

            @pl.when(is_kind(k) & jnp.logical_not(last))
            def _():
                out_ref[...] = (own_ref[...] + term_ref[...].astype(F32)).astype(BF16)

            @pl.when(is_kind(k) & last)
            def _():
                out_ref[...] = own_ref[...].astype(BF16)

            if k:

                @pl.when(is_kind(0))
                def _():
                    out_ref[...] = source_ref[...]

        return call(kernel, [VM, VM, VM if k else ANY], [block], SHORT, size, own, term_next[k], source)[0]

    imag_sum = imag_part(1, imag_part(0, real_sum))

    def finish(factor_ref, imag_ref, real_ref, *refs):
        got, out_ref, held_ref, sems = refs[: rounds - 1], refs[-3], refs[-2], refs[-1]
        imag_copy = pltpu.make_async_copy(imag_ref, out_ref.at[0, 0, 1], sems.at[1])
        imag_copy.start()
        total = real_ref[...]
        for r, ref in enumerate(got, 1):
            total += scaled(ref, factor_ref, r)
        held_ref[...] = total.astype(BF16)
        real_copy = pltpu.make_async_copy(held_ref, out_ref.at[0, 0, 0], sems.at[0])
        real_copy.start()
        imag_copy.wait()
        real_copy.wait()

    return pl.pallas_call(
        finish,
        out_shape=jax.ShapeDtypeStruct(green.shape, BF16),
        in_specs=[VM] * (2 + rounds),
        out_specs=ANY,
        scratch_shapes=[block, pltpu.SemaphoreType.DMA((2,))],
        compiler_params=pltpu.CompilerParams(vmem_limit_bytes=24 << 20),
    )(factors, imag_sum, real_sum, *arrived[1:])


def solution(mesh):
    count, slabs = mesh.shape["energy"], mesh.shape["slab"]
    placed = (P("energy", "slab", None, None, None), P("energy", None, None), P(), P())
    return jax.shard_map(
        functools.partial(body, count, slabs, matchings(count)),
        mesh=mesh,
        in_specs=placed,
        out_specs=P("energy", "slab", None, None, None),
        check_vma=False,
    )
```

```python
import functools

import jax
import jax.numpy as jnp
from jax import lax
from jax.experimental import pallas as pl
from jax.experimental.pallas import tpu as pltpu
from jax.sharding import PartitionSpec as P

SHIFTS = (3, 7)
KINDS = (1, 0)
LONG = 400
SHORT = 2
F32, BF16 = jnp.float32, jnp.bfloat16
NT = (((1,), (1,)), ((), ()))


def matchings(count):
    left = {}
    for target in range(count):
        for mode, shift in enumerate(SHIFTS):
            for side, source in enumerate((target + shift, target - shift)):
                if 0 <= source < count:
                    left[source, target] = (mode, side)
    rounds = []
    while left:
        options = {}
        for source, target in sorted(left):
            options.setdefault(source, []).append(target)
        taken = {}

        def place(source, seen):
            for target in options[source]:
                if target not in seen:
                    seen.add(target)
                    if target not in taken or place(taken[target], seen):
                        taken[target] = source
                        return True
            return False

        for source in sorted(options):
            place(source, set())
        rounds.append({t: (s,) + left.pop((s, t)) for t, s in sorted(taken.items())})
    return rounds


def lookup(table, index):
    value = jnp.int32(table[0])
    for start in range(len(table)):
        if start and table[start] != table[start - 1]:
            value = jnp.where(index >= start, jnp.int32(table[start]), value)
    return value


def routes(plan, count):
    out = []
    for step in plan:
        took, gave = [0] * count, [0] * count
        for target, (source, mode, side) in step.items():
            took[target] = 1 + mode * 2 + side
            gave[source] = mode
        out.append((took, gave))
    return out


def arriving(route):
    code = lookup(route[0], lax.axis_index("energy"))
    slot = jnp.maximum(code - 1, 0)
    return slot // 2, slot % 2, code > 0


def descent(count, slabs, kind):
    pairs = []
    for e in range(count):
        if e ^ 1 >= count and e % 2 != kind:
            continue
        for s in range(slabs):
            to = s - 1 if e % 2 == kind else s + 1
            if 0 <= to < slabs:
                pairs.append((e * slabs + s, e * slabs + to))
            elif e ^ 1 < count:
                pairs.append((e * slabs + s, (e ^ 1) * slabs + s))
    return pairs


def closed(step, count):
    sources = {source for source, _, _ in step.values()}
    return count % 2 == 0 and sources == set(step) and all((e in step) != (e + 1 in step) for e in range(0, count, 2))


def dot(a, b):
    return jnp.dot(a, b, preferred_element_type=F32)


def dot_t(a, b):
    return lax.dot_general(a, b, NT, preferred_element_type=F32)


def couple(mat, x):
    return dot_t(dot(mat, x).astype(BF16), mat)


VM = pl.BlockSpec(memory_space=pltpu.VMEM)
SM = pl.BlockSpec(memory_space=pltpu.SMEM)
ANY = pl.BlockSpec(memory_space=pl.ANY)


def call(kernel, ins, outs, products, size, *args, scratch=()):
    return pl.pallas_call(
        kernel,
        out_shape=outs,
        in_specs=ins,
        out_specs=[VM] * len(outs),
        scratch_shapes=scratch,
        cost_estimate=pl.CostEstimate(flops=2 * products * size**3, bytes_accessed=1 << 20, transcendentals=0),
        compiler_params=pltpu.CompilerParams(vmem_limit_bytes=24 << 20),
    )(*args)


def body(count, slabs, plan, green, weights, coupling_m, coupling_n):
    size = green.shape[-1]
    block = pltpu.VMEM((size, size), BF16)
    wide = pltpu.VMEM((size, size), F32)
    rounds = len(plan)
    route = routes(plan, count)

    def split(green_ref, real_ref, imag_ref, sems):
        copies = [
            pltpu.make_async_copy(green_ref.at[0, 0, part], out, sems.at[part])
            for part, out in enumerate((real_ref, imag_ref))
        ]
        for copy in copies:
            copy.start()
        for copy in copies:
            copy.wait()

    real, imag = pl.pallas_call(
        split,
        out_shape=[block, block],
        in_specs=[ANY],
        out_specs=[VM, VM],
        scratch_shapes=[pltpu.SemaphoreType.DMA((2,))],
    )(green)

    def along(x, step):
        return lax.ppermute(x, "energy", [(s, t) for t, (s, _, _) in step.items()])

    def along_closed(x, step):
        if not closed(step, count):
            return along(x, step)
        swapped = lax.ppermute(x, "energy", [(e, e ^ 1) for e in range(count)])
        pairs = [(s ^ 1, t) for t, (s, _, _) in step.items()] + [(t, t ^ 1) for t in step]
        return lax.ppermute(swapped, "energy", pairs)

    def from_next(x):
        return [lax.ppermute(x, ("energy", "slab"), descent(count, slabs, kind)) for kind in KINDS]

    def sent_mode(r):
        return lookup(route[r][1], lax.axis_index("energy"))

    near = [along(imag, step) for step in plan]
    behind = from_next(real)

    def first(weights_ref, real_ref, cm_ref, cn_ref, factor_ref, near_ref, *rest):
        outs, sem = rest[:-1], rest[-1]
        copy = pltpu.make_async_copy(cn_ref, near_ref, sem)
        copy.start()
        for r, out in enumerate(outs):
            mode, side, present = arriving(route[r])
            factor = jnp.where(present, weights_ref[0, mode, side], 0).astype(F32) / 32.0
            factor_ref[r] = jnp.full((8, size), factor, F32)
            out[...] = couple(cm_ref[sent_mode(r)], real_ref[...])
        copy.wait()

    factors, coupling_n, *partial = call(
        first,
        [SM, VM, VM, ANY],
        [pltpu.VMEM((rounds, 8, size), F32), pltpu.VMEM(coupling_n.shape, BF16)] + [wide] * rounds,
        2 * rounds,
        size,
        weights,
        real,
        coupling_m,
        pltpu.with_memory_space_constraint(coupling_n, pltpu.HBM),
        scratch=[pltpu.SemaphoreType.DMA],
    )

    def scaled(ref, factor_ref, r):
        return factor_ref[r, 0:1, :] * ref[...].astype(F32)

    def is_kind(k):
        return lax.axis_index("energy") % 2 == KINDS[k]

    def own_result(r):
        sources = {source: mode for source, mode, _ in plan[r].values()}
        return lookup([int(e in sources and sources[e] != route[0][1][e]) for e in range(count)], lax.axis_index("energy"))

    def result(r, partial_ref, behind_ref, cn_ref, out_ref):
        here = lax.axis_index("slab") < slabs - 1

        @pl.when(here)
        def _():
            out_ref[...] = (partial_ref[...] + couple(cn_ref[sent_mode(r)], behind_ref[...])).astype(BF16)

        @pl.when(jnp.logical_not(here))
        def _():
            out_ref[...] = partial_ref[...].astype(BF16)

    def later_result(r, partial_ref, behind_ref, cn_ref, first_ref, out_ref):
        again = own_result(r) == 0

        @pl.when(again)
        def _():
            out_ref[...] = first_ref[...]

        @pl.when(jnp.logical_not(again))
        def _():
            result(r, partial_ref, behind_ref, cn_ref, out_ref)

    def early(behind_ref, cn_ref, *refs):
        parts, outs = refs[:rounds], refs[rounds:]

        @pl.when(is_kind(0))
        def _():
            result(0, parts[0], behind_ref, cn_ref, outs[0])
            for r in range(1, rounds):
                later_result(r, parts[r], behind_ref, cn_ref, outs[0], outs[r])

    ready = call(early, [VM] * (2 + rounds), [block] * rounds, 2, size, behind[0], coupling_n, *partial)

    def late(behind_ref, cn_ref, partial_ref, ready_ref, out_ref):
        @pl.when(is_kind(0))
        def _():
            out_ref[...] = ready_ref[...]

        @pl.when(is_kind(1))
        def _():
            result(0, partial_ref, behind_ref, cn_ref, out_ref)

    results = call(late, [VM] * 4, [block], 2, size, behind[1], coupling_n, partial[0], ready[0])
    arrived = [along(results[0], plan[0])]

    def late_rest(behind_ref, cn_ref, first_ref, *refs):
        for r in range(1, rounds):
            part, done, out = (refs[r - 1 + k * (rounds - 1)] for k in range(3))

            @pl.when(is_kind(0))
            def _():
                out[...] = done[...]

            @pl.when(is_kind(1))
            def _():
                later_result(r, part, behind_ref, cn_ref, first_ref, out)

    if rounds > 1:
        results = list(results) + list(
            call(
                late_rest,
                [VM] * (3 + 2 * (rounds - 1)),
                [block] * (rounds - 1),
                2,
                size,
                behind[1],
                coupling_n,
                results[0],
                *partial[1:],
                *ready[1:],
            )
        )
        arrived += [along_closed(results[r], plan[r]) for r in range(1, rounds)]

    def arrivals():
        modes, present = zip(*[(mode, there) for mode, _, there in map(arriving, route)])
        ahead = lax.axis_index("slab") > 0
        return modes, [ahead & there for there in present]

    def term_first(factor_ref, cn_ref, after_ref, got_ref, left_ref, whole_ref):
        modes, present = arrivals()
        follows = present[1] if rounds > 1 else False
        mat = cn_ref[modes[0]]

        @pl.when(present[0])
        def _():
            left_ref[...] = dot(mat, scaled(got_ref, factor_ref, 0).astype(BF16)).astype(BF16)

        @pl.when(present[0] & jnp.logical_not(follows))
        def _():
            whole_ref[...] = dot_t(left_ref[...], mat)

    left, begun = call(
        term_first, [VM, VM, ANY, VM], [block, wide], 2, size, factors, coupling_n, results[-1], near[0]
    )

    def term_sum(factor_ref, cn_ref, left_ref, begun_ref, *refs):
        got, out_ref, total_ref, side_ref = refs[: rounds - 1], refs[-3], refs[-2], refs[-1]
        modes, present = arrivals()
        follows = present[1] if rounds > 1 else jnp.bool_(False)

        def left_of(r):
            return dot(cn_ref[modes[r]], scaled(got[r - 1], factor_ref, r).astype(BF16)).astype(BF16)

        @pl.when(present[0] & jnp.logical_not(follows))
        def _():
            total_ref[...] = begun_ref[...]

        @pl.when(jnp.logical_not(present[0] | follows))
        def _():
            total_ref[...] = jnp.zeros_like(total_ref)

        if rounds > 1:
            @pl.when(present[0] & follows)
            def _():
                side_ref[:, :size] = left_ref[...]
                side_ref[:, size:] = left_of(1)
                mats = jnp.concatenate([cn_ref[modes[0]], cn_ref[modes[1]]], 1)
                total_ref[...] = dot_t(side_ref[...], mats)

            @pl.when(jnp.logical_not(present[0]) & follows)
            def _():
                total_ref[...] = dot_t(left_of(1), cn_ref[modes[1]])

        for r in range(2, rounds):

            @pl.when(present[r])
            def _():
                total_ref[...] += dot_t(left_of(r), cn_ref[modes[r]])

        out_ref[...] = total_ref[...].astype(BF16)

    (term,) = call(
        term_sum,
        [VM] * (4 + rounds - 1),
        [block],
        LONG,
        size,
        factors,
        coupling_n,
        left,
        begun,
        *near[1:],
        scratch=[wide, pltpu.VMEM((size, 2 * size), BF16)],
    )
    term_next = from_next(term)

    def own_sum(factor_ref, cm_ref, after_ref, *refs):
        got, out_ref = refs[:-1], refs[-1]
        out_ref[...] = jnp.zeros_like(out_ref)
        for r, ref in enumerate(got):
            mode, _, present = arriving(route[r])

            @pl.when(present)
            def _():
                out_ref[...] += couple(cm_ref[mode], scaled(ref, factor_ref, r).astype(BF16))

    (own,) = call(
        own_sum, [VM, VM, ANY] + [VM] * rounds, [wide], 2 * rounds, size, factors, coupling_m, term, *near
    )

    def real_first(factor_ref, got_ref, out_ref):
        out_ref[...] = scaled(got_ref, factor_ref, 0)

    (real_sum,) = call(real_first, [VM, VM], [wide], SHORT, size, factors, arrived[0])

    def imag_part(k, source):
        def kernel(own_ref, term_ref, source_ref, out_ref):
            last = lax.axis_index("slab") == slabs - 1

            @pl.when(is_kind(k) & jnp.logical_not(last))
            def _():
                out_ref[...] = (own_ref[...] + term_ref[...].astype(F32)).astype(BF16)

            @pl.when(is_kind(k) & last)
            def _():
                out_ref[...] = own_ref[...].astype(BF16)

        return call(kernel, [VM, VM, ANY], [block], SHORT, size, own, term_next[k], source)[0]

    imag_sum = imag_part(0, real_sum)

    def finish(factor_ref, own_ref, term_ref, imag_ref, real_ref, *refs):
        got, out_ref, held_ref, made_ref, sems = refs[: rounds - 1], refs[-4], refs[-3], refs[-2], refs[-1]
        last = lax.axis_index("slab") == slabs - 1

        def imag_copy(ref):
            return pltpu.make_async_copy(ref, out_ref.at[0, 0, 1], sems.at[1])

        @pl.when(is_kind(0))
        def _():
            imag_copy(imag_ref).start()

        @pl.when(is_kind(1) & jnp.logical_not(last))
        def _():
            made_ref[...] = (own_ref[...] + term_ref[...].astype(F32)).astype(BF16)

        @pl.when(is_kind(1) & last)
        def _():
            made_ref[...] = own_ref[...].astype(BF16)

        @pl.when(is_kind(1))
        def _():
            imag_copy(made_ref).start()

        total = real_ref[...]
        for r, ref in enumerate(got, 1):
            total += scaled(ref, factor_ref, r)
        held_ref[...] = total.astype(BF16)
        real_copy = pltpu.make_async_copy(held_ref, out_ref.at[0, 0, 0], sems.at[0])
        real_copy.start()
        imag_copy(made_ref).wait()
        real_copy.wait()

    return pl.pallas_call(
        finish,
        out_shape=jax.ShapeDtypeStruct(green.shape, BF16),
        in_specs=[VM] * (4 + rounds),
        out_specs=ANY,
        scratch_shapes=[block, block, pltpu.SemaphoreType.DMA((2,))],
        compiler_params=pltpu.CompilerParams(vmem_limit_bytes=24 << 20),
    )(factors, own, term_next[1], imag_sum, real_sum, *arrived[1:])


def solution(mesh):
    count, slabs = mesh.shape["energy"], mesh.shape["slab"]
    placed = (P("energy", "slab", None, None, None), P("energy", None, None), P(), P())
    return jax.shard_map(
        functools.partial(body, count, slabs, matchings(count)),
        mesh=mesh,
        in_specs=placed,
        out_specs=P("energy", "slab", None, None, None),
        check_vma=False,
    )
```

```python
import functools

import jax
import jax.numpy as jnp
from jax import lax
from jax.experimental import pallas as pl
from jax.experimental.pallas import tpu as pltpu
from jax.sharding import PartitionSpec as P

SHIFTS = (3, 7)
KINDS = (1, 0)
LONG = 400
SHORT = 2
F32, BF16 = jnp.float32, jnp.bfloat16
NT = (((1,), (1,)), ((), ()))


def matchings(count):
    left = {}
    for target in range(count):
        for mode, shift in enumerate(SHIFTS):
            for side, source in enumerate((target + shift, target - shift)):
                if 0 <= source < count:
                    left[source, target] = (mode, side)
    rounds = []
    while left:
        options = {}
        for source, target in sorted(left):
            options.setdefault(source, []).append(target)
        taken = {}

        def place(source, seen):
            for target in options[source]:
                if target not in seen:
                    seen.add(target)
                    if target not in taken or place(taken[target], seen):
                        taken[target] = source
                        return True
            return False

        for source in sorted(options):
            place(source, set())
        rounds.append({t: (s,) + left.pop((s, t)) for t, s in sorted(taken.items())})
    return rounds


def lookup(table, index):
    value = jnp.int32(table[0])
    for start in range(len(table)):
        if start and table[start] != table[start - 1]:
            value = jnp.where(index >= start, jnp.int32(table[start]), value)
    return value


def routes(plan, count):
    out = []
    for step in plan:
        took, gave = [0] * count, [0] * count
        for target, (source, mode, side) in step.items():
            took[target] = 1 + mode * 2 + side
            gave[source] = mode
        out.append((took, gave))
    return out


def arriving(route):
    code = lookup(route[0], lax.axis_index("energy"))
    slot = jnp.maximum(code - 1, 0)
    return slot // 2, slot % 2, code > 0


def descent(count, slabs, kind):
    pairs = []
    for e in range(count):
        if e ^ 1 >= count and e % 2 != kind:
            continue
        for s in range(slabs):
            to = s - 1 if e % 2 == kind else s + 1
            if 0 <= to < slabs:
                pairs.append((e * slabs + s, e * slabs + to))
            elif e ^ 1 < count:
                pairs.append((e * slabs + s, (e ^ 1) * slabs + s))
    return pairs


def closed(step, count):
    sources = {source for source, _, _ in step.values()}
    return count % 2 == 0 and sources == set(step) and all((e in step) != (e + 1 in step) for e in range(0, count, 2))


def dot(a, b):
    return jnp.dot(a, b, preferred_element_type=F32)


def dot_t(a, b):
    return lax.dot_general(a, b, NT, preferred_element_type=F32)


def couple(mat, x):
    return dot_t(dot(mat, x).astype(BF16), mat)


VM = pl.BlockSpec(memory_space=pltpu.VMEM)
SM = pl.BlockSpec(memory_space=pltpu.SMEM)
ANY = pl.BlockSpec(memory_space=pl.ANY)


def call(kernel, ins, outs, products, size, *args, scratch=()):
    return pl.pallas_call(
        kernel,
        out_shape=outs,
        in_specs=ins,
        out_specs=[VM] * len(outs),
        scratch_shapes=scratch,
        cost_estimate=pl.CostEstimate(flops=2 * products * size**3, bytes_accessed=1 << 20, transcendentals=0),
        compiler_params=pltpu.CompilerParams(vmem_limit_bytes=24 << 20),
    )(*args)


def body(count, slabs, plan, green, weights, coupling_m, coupling_n):
    size = green.shape[-1]
    block = pltpu.VMEM((size, size), BF16)
    wide = pltpu.VMEM((size, size), F32)
    rounds = len(plan)
    route = routes(plan, count)

    def split(green_ref, real_ref, sem):
        copy = pltpu.make_async_copy(green_ref.at[0, 0, 0], real_ref, sem)
        copy.start()
        copy.wait()

    (real,) = call(split, [ANY], [block], 1, size, pltpu.with_memory_space_constraint(green, pltpu.HBM), scratch=[pltpu.SemaphoreType.DMA])

    def second_part(green_ref, after_ref, imag_ref):
        imag_ref[...] = green_ref[0, 0, 1]

    (imag,) = call(second_part, [VM, ANY], [block], 1, size, green, real)

    def along(x, step):
        return lax.ppermute(x, "energy", [(s, t) for t, (s, _, _) in step.items()])

    def along_closed(x, step):
        if not closed(step, count):
            return along(x, step)
        swapped = lax.ppermute(x, "energy", [(e, e ^ 1) for e in range(count)])
        pairs = [(s ^ 1, t) for t, (s, _, _) in step.items()] + [(t, t ^ 1) for t in step]
        return lax.ppermute(swapped, "energy", pairs)

    def from_next(x):
        return [lax.ppermute(x, ("energy", "slab"), descent(count, slabs, kind)) for kind in KINDS]

    def sent_mode(r):
        return lookup(route[r][1], lax.axis_index("energy"))

    near = [along(imag, step) for step in plan]
    behind = from_next(real)

    def first(weights_ref, real_ref, cm_ref, cn_ref, factor_ref, near_ref, *rest):
        outs, sem = rest[:-1], rest[-1]
        copy = pltpu.make_async_copy(cn_ref, near_ref, sem)
        copy.start()
        for r, out in enumerate(outs):
            mode, side, present = arriving(route[r])
            factor = jnp.where(present, weights_ref[0, mode, side], 0).astype(F32) / 32.0
            factor_ref[r] = jnp.full((8, size), factor, F32)
            out[...] = couple(cm_ref[sent_mode(r)], real_ref[...])
        copy.wait()

    factors, coupling_n, *partial = call(
        first,
        [SM, VM, VM, ANY],
        [pltpu.VMEM((rounds, 8, size), F32), pltpu.VMEM(coupling_n.shape, BF16)] + [wide] * rounds,
        2 * rounds,
        size,
        weights,
        real,
        coupling_m,
        pltpu.with_memory_space_constraint(coupling_n, pltpu.HBM),
        scratch=[pltpu.SemaphoreType.DMA],
    )

    def scaled(ref, factor_ref, r):
        return factor_ref[r, 0:1, :] * ref[...].astype(F32)

    def is_kind(k):
        return lax.axis_index("energy") % 2 == KINDS[k]

    def own_result(r):
        sources = {source: mode for source, mode, _ in plan[r].values()}
        return lookup([int(e in sources and sources[e] != route[0][1][e]) for e in range(count)], lax.axis_index("energy"))

    def result(r, partial_ref, behind_ref, cn_ref, out_ref):
        here = lax.axis_index("slab") < slabs - 1

        @pl.when(here)
        def _():
            out_ref[...] = (partial_ref[...] + couple(cn_ref[sent_mode(r)], behind_ref[...])).astype(BF16)

        @pl.when(jnp.logical_not(here))
        def _():
            out_ref[...] = partial_ref[...].astype(BF16)

    def later_result(r, partial_ref, behind_ref, cn_ref, first_ref, out_ref):
        again = own_result(r) == 0

        @pl.when(again)
        def _():
            out_ref[...] = first_ref[...]

        @pl.when(jnp.logical_not(again))
        def _():
            result(r, partial_ref, behind_ref, cn_ref, out_ref)

    def early(behind_ref, cn_ref, *refs):
        parts, outs = refs[:rounds], refs[rounds:]

        @pl.when(is_kind(0))
        def _():
            result(0, parts[0], behind_ref, cn_ref, outs[0])
            for r in range(1, rounds):
                later_result(r, parts[r], behind_ref, cn_ref, outs[0], outs[r])

    ready = call(early, [VM] * (2 + rounds), [block] * rounds, 2, size, behind[0], coupling_n, *partial)

    def late(behind_ref, cn_ref, partial_ref, ready_ref, out_ref):
        @pl.when(is_kind(0))
        def _():
            out_ref[...] = ready_ref[...]

        @pl.when(is_kind(1))
        def _():
            result(0, partial_ref, behind_ref, cn_ref, out_ref)

    results = call(late, [VM] * 4, [block], 2, size, behind[1], coupling_n, partial[0], ready[0])
    arrived = [along(results[0], plan[0])]

    def late_rest(behind_ref, cn_ref, first_ref, *refs):
        for r in range(1, rounds):
            part, done, out = (refs[r - 1 + k * (rounds - 1)] for k in range(3))

            @pl.when(is_kind(0))
            def _():
                out[...] = done[...]

            @pl.when(is_kind(1))
            def _():
                later_result(r, part, behind_ref, cn_ref, first_ref, out)

    if rounds > 1:
        results = list(results) + list(
            call(
                late_rest,
                [VM] * (3 + 2 * (rounds - 1)),
                [block] * (rounds - 1),
                2,
                size,
                behind[1],
                coupling_n,
                results[0],
                *partial[1:],
                *ready[1:],
            )
        )
        arrived += [along_closed(results[r], plan[r]) for r in range(1, rounds)]

    def term_first(factor_ref, cn_ref, got_ref, after_ref, out_ref):
        mode, _, present = arriving(route[0])
        ahead = lax.axis_index("slab") > 0

        @pl.when(present & ahead)
        def _():
            out_ref[...] = couple(cn_ref[mode], scaled(got_ref, factor_ref, 0).astype(BF16))

        @pl.when(jnp.logical_not(present & ahead))
        def _():
            out_ref[...] = jnp.zeros_like(out_ref)

    (begun,) = call(term_first, [VM, VM, VM, ANY], [wide], 2, size, factors, coupling_n, near[0], results[-1])

    def term_rest(factor_ref, cn_ref, after_ref, begun_ref, *refs):
        got, out_ref, total_ref = refs[:-2], refs[-2], refs[-1]
        total_ref[...] = begun_ref[...]
        for r, ref in enumerate(got, 1):
            mode, _, present = arriving(route[r])

            @pl.when(present & (lax.axis_index("slab") > 0))
            def _():
                total_ref[...] += couple(cn_ref[mode], scaled(ref, factor_ref, r).astype(BF16))

        out_ref[...] = total_ref[...].astype(BF16)

    (term,) = call(
        term_rest,
        [VM, VM, ANY, VM] + [VM] * (rounds - 1),
        [block],
        LONG,
        size,
        factors,
        coupling_n,
        results[-1],
        begun,
        *near[1:],
        scratch=[wide],
    )
    term_next = from_next(term)

    def own_sum(factor_ref, cm_ref, after_ref, *refs):
        got, out_ref = refs[:-1], refs[-1]
        out_ref[...] = jnp.zeros_like(out_ref)
        for r, ref in enumerate(got):
            mode, _, present = arriving(route[r])

            @pl.when(present)
            def _():
                out_ref[...] += couple(cm_ref[mode], scaled(ref, factor_ref, r).astype(BF16))

    (own,) = call(
        own_sum, [VM, VM, ANY] + [VM] * rounds, [wide], 2 * rounds, size, factors, coupling_m, term, *near
    )

    def real_first(factor_ref, got_ref, out_ref):
        out_ref[...] = scaled(got_ref, factor_ref, 0)

    (real_sum,) = call(real_first, [VM, VM], [wide], SHORT, size, factors, arrived[0])

    def imag_part(k, source):
        def kernel(own_ref, term_ref, source_ref, out_ref):
            last = lax.axis_index("slab") == slabs - 1

            @pl.when(is_kind(k) & jnp.logical_not(last))
            def _():
                out_ref[...] = (own_ref[...] + term_ref[...].astype(F32)).astype(BF16)

            @pl.when(is_kind(k) & last)
            def _():
                out_ref[...] = own_ref[...].astype(BF16)

        return call(kernel, [VM, VM, ANY], [block], SHORT, size, own, term_next[k], source)[0]

    imag_sum = imag_part(0, real_sum)

    def finish(factor_ref, own_ref, term_ref, imag_ref, real_ref, *refs):
        got, out_ref, held_ref, made_ref, sems = refs[: rounds - 1], refs[-4], refs[-3], refs[-2], refs[-1]
        last = lax.axis_index("slab") == slabs - 1

        def imag_copy(ref):
            return pltpu.make_async_copy(ref, out_ref.at[0, 0, 1], sems.at[1])

        @pl.when(is_kind(0))
        def _():
            imag_copy(imag_ref).start()

        @pl.when(is_kind(1) & jnp.logical_not(last))
        def _():
            made_ref[...] = (own_ref[...] + term_ref[...].astype(F32)).astype(BF16)

        @pl.when(is_kind(1) & last)
        def _():
            made_ref[...] = own_ref[...].astype(BF16)

        @pl.when(is_kind(1))
        def _():
            imag_copy(made_ref).start()

        total = real_ref[...]
        for r, ref in enumerate(got, 1):
            total += scaled(ref, factor_ref, r)
        held_ref[...] = total.astype(BF16)
        real_copy = pltpu.make_async_copy(held_ref, out_ref.at[0, 0, 0], sems.at[0])
        real_copy.start()
        imag_copy(made_ref).wait()
        real_copy.wait()

    return pl.pallas_call(
        finish,
        out_shape=jax.ShapeDtypeStruct(green.shape, BF16),
        in_specs=[VM] * (4 + rounds),
        out_specs=ANY,
        scratch_shapes=[block, block, pltpu.SemaphoreType.DMA((2,))],
        compiler_params=pltpu.CompilerParams(vmem_limit_bytes=24 << 20),
    )(factors, own, term_next[1], imag_sum, real_sum, *arrived[1:])


def solution(mesh):
    count, slabs = mesh.shape["energy"], mesh.shape["slab"]
    placed = (P("energy", "slab", None, None, None), P("energy", None, None), P(), P())
    return jax.shard_map(
        functools.partial(body, count, slabs, matchings(count)),
        mesh=mesh,
        in_specs=placed,
        out_specs=P("energy", "slab", None, None, None),
        check_vma=False,
    )
```

```python
import functools

import jax
import jax.numpy as jnp
from jax import lax
from jax.experimental import pallas as pl
from jax.experimental.pallas import tpu as pltpu
from jax.sharding import PartitionSpec as P

SHIFTS = (3, 7)
KINDS = (1, 0)
LONG = 400
SHORT = 2
F32, BF16 = jnp.float32, jnp.bfloat16
NT = (((1,), (1,)), ((), ()))


def matchings(count):
    left = {}
    for target in range(count):
        for mode, shift in enumerate(SHIFTS):
            for side, source in enumerate((target + shift, target - shift)):
                if 0 <= source < count:
                    left[source, target] = (mode, side)
    rounds = []
    while left:
        options = {}
        for source, target in sorted(left):
            options.setdefault(source, []).append(target)
        taken = {}

        def place(source, seen):
            for target in options[source]:
                if target not in seen:
                    seen.add(target)
                    if target not in taken or place(taken[target], seen):
                        taken[target] = source
                        return True
            return False

        for source in sorted(options):
            place(source, set())
        rounds.append({t: (s,) + left.pop((s, t)) for t, s in sorted(taken.items())})
    return rounds


def lookup(table, index):
    value = jnp.int32(table[0])
    for start in range(len(table)):
        if start and table[start] != table[start - 1]:
            value = jnp.where(index >= start, jnp.int32(table[start]), value)
    return value


def routes(plan, count):
    out = []
    for step in plan:
        took, gave = [0] * count, [0] * count
        for target, (source, mode, side) in step.items():
            took[target] = 1 + mode * 2 + side
            gave[source] = mode
        out.append((took, gave))
    return out


def arriving(route):
    code = lookup(route[0], lax.axis_index("energy"))
    slot = jnp.maximum(code - 1, 0)
    return slot // 2, slot % 2, code > 0


def descent(count, slabs, kind):
    pairs = []
    for e in range(count):
        if e ^ 1 >= count and e % 2 != kind:
            continue
        for s in range(slabs):
            to = s - 1 if e % 2 == kind else s + 1
            if 0 <= to < slabs:
                pairs.append((e * slabs + s, e * slabs + to))
            elif e ^ 1 < count:
                pairs.append((e * slabs + s, (e ^ 1) * slabs + s))
    return pairs


def closed(step, count):
    sources = {source for source, _, _ in step.values()}
    return count % 2 == 0 and sources == set(step) and all((e in step) != (e + 1 in step) for e in range(0, count, 2))


def dot(a, b):
    return jnp.dot(a, b, preferred_element_type=F32)


def dot_t(a, b):
    return lax.dot_general(a, b, NT, preferred_element_type=F32)


def couple(mat, x):
    return dot_t(dot(mat, x).astype(BF16), mat)


VM = pl.BlockSpec(memory_space=pltpu.VMEM)
SM = pl.BlockSpec(memory_space=pltpu.SMEM)
ANY = pl.BlockSpec(memory_space=pl.ANY)


def call(kernel, ins, outs, products, size, *args, scratch=()):
    return pl.pallas_call(
        kernel,
        out_shape=outs,
        in_specs=ins,
        out_specs=[VM] * len(outs),
        scratch_shapes=scratch,
        cost_estimate=pl.CostEstimate(flops=2 * products * size**3, bytes_accessed=1 << 20, transcendentals=0),
        compiler_params=pltpu.CompilerParams(vmem_limit_bytes=24 << 20),
    )(*args)


def body(count, slabs, plan, green, weights, coupling_m, coupling_n):
    size = green.shape[-1]
    block = pltpu.VMEM((size, size), BF16)
    wide = pltpu.VMEM((size, size), F32)
    rounds = len(plan)
    route = routes(plan, count)

    def split(green_ref, real_ref, imag_ref, sems):
        copies = [
            pltpu.make_async_copy(green_ref.at[0, 0, part], out, sems.at[part])
            for part, out in enumerate((real_ref, imag_ref))
        ]
        for copy in copies:
            copy.start()
        for copy in copies:
            copy.wait()

    real, imag = pl.pallas_call(
        split,
        out_shape=[block, block],
        in_specs=[ANY],
        out_specs=[VM, VM],
        scratch_shapes=[pltpu.SemaphoreType.DMA((2,))],
    )(green)

    def along(x, step):
        return lax.ppermute(x, "energy", [(s, t) for t, (s, _, _) in step.items()])

    def along_closed(x, step):
        if not closed(step, count):
            return along(x, step)
        swapped = lax.ppermute(x, "energy", [(e, e ^ 1) for e in range(count)])
        pairs = [(s ^ 1, t) for t, (s, _, _) in step.items()] + [(t, t ^ 1) for t in step]
        return lax.ppermute(swapped, "energy", pairs)

    def from_next(x):
        return [lax.ppermute(x, ("energy", "slab"), descent(count, slabs, kind)) for kind in KINDS]

    def sent_mode(r):
        return lookup(route[r][1], lax.axis_index("energy"))

    near = [along(imag, step) for step in plan]
    behind = from_next(real)

    def first(weights_ref, real_ref, cm_ref, cn_ref, factor_ref, near_ref, *rest):
        outs, sem = rest[:-1], rest[-1]
        copy = pltpu.make_async_copy(cn_ref, near_ref, sem)
        copy.start()
        for r, out in enumerate(outs):
            mode, side, present = arriving(route[r])
            factor = jnp.where(present, weights_ref[0, mode, side], 0).astype(F32) / 32.0
            factor_ref[r] = jnp.full((8, size), factor, F32)
            out[...] = couple(cm_ref[sent_mode(r)], real_ref[...])
        copy.wait()

    factors, coupling_n, *partial = call(
        first,
        [SM, VM, VM, ANY],
        [pltpu.VMEM((rounds, 8, size), F32), pltpu.VMEM(coupling_n.shape, BF16)] + [wide] * rounds,
        2 * rounds,
        size,
        weights,
        real,
        coupling_m,
        pltpu.with_memory_space_constraint(coupling_n, pltpu.HBM),
        scratch=[pltpu.SemaphoreType.DMA],
    )

    def scaled(ref, factor_ref, r):
        return factor_ref[r, 0:1, :] * ref[...].astype(F32)

    def is_kind(k):
        return lax.axis_index("energy") % 2 == KINDS[k]

    def own_result(r):
        sources = {source: mode for source, mode, _ in plan[r].values()}
        return lookup([int(e in sources and sources[e] != route[0][1][e]) for e in range(count)], lax.axis_index("energy"))

    def result(r, partial_ref, behind_ref, cn_ref, out_ref):
        here = lax.axis_index("slab") < slabs - 1

        @pl.when(here)
        def _():
            out_ref[...] = (partial_ref[...] + couple(cn_ref[sent_mode(r)], behind_ref[...])).astype(BF16)

        @pl.when(jnp.logical_not(here))
        def _():
            out_ref[...] = partial_ref[...].astype(BF16)

    def later_result(r, partial_ref, behind_ref, cn_ref, first_ref, out_ref):
        again = own_result(r) == 0

        @pl.when(again)
        def _():
            out_ref[...] = first_ref[...]

        @pl.when(jnp.logical_not(again))
        def _():
            result(r, partial_ref, behind_ref, cn_ref, out_ref)

    def early(behind_ref, cn_ref, *refs):
        parts, outs = refs[:rounds], refs[rounds:]

        @pl.when(is_kind(0))
        def _():
            result(0, parts[0], behind_ref, cn_ref, outs[0])
            for r in range(1, rounds):
                later_result(r, parts[r], behind_ref, cn_ref, outs[0], outs[r])

    ready = call(early, [VM] * (2 + rounds), [block] * rounds, 2, size, behind[0], coupling_n, *partial)

    def late(behind_ref, cn_ref, partial_ref, ready_ref, out_ref):
        @pl.when(is_kind(0))
        def _():
            out_ref[...] = ready_ref[...]

        @pl.when(is_kind(1))
        def _():
            result(0, partial_ref, behind_ref, cn_ref, out_ref)

    results = call(late, [VM] * 4, [block], 2, size, behind[1], coupling_n, partial[0], ready[0])
    arrived = [along(results[0], plan[0])]

    def late_rest(behind_ref, cn_ref, first_ref, *refs):
        for r in range(1, rounds):
            part, done, out = (refs[r - 1 + k * (rounds - 1)] for k in range(3))

            @pl.when(is_kind(0))
            def _():
                out[...] = done[...]

            @pl.when(is_kind(1))
            def _():
                later_result(r, part, behind_ref, cn_ref, first_ref, out)

    if rounds > 1:
        results = list(results) + list(
            call(
                late_rest,
                [VM] * (3 + 2 * (rounds - 1)),
                [block] * (rounds - 1),
                2,
                size,
                behind[1],
                coupling_n,
                results[0],
                *partial[1:],
                *ready[1:],
            )
        )
        arrived += [along_closed(results[r], plan[r]) for r in range(1, rounds)]

    def term_sum(factor_ref, cn_ref, after_ref, *refs):
        got, out_ref, total_ref, left_ref = refs[:rounds], refs[-3], refs[-2], refs[-1]
        ahead = lax.axis_index("slab") > 0
        modes, present = zip(*[(mode, there) for mode, _, there in map(arriving, route)])

        def left(r):
            return dot(cn_ref[modes[r]], scaled(got[r], factor_ref, r).astype(BF16)).astype(BF16)

        both = ahead & present[0] & present[1] if rounds > 1 else False
        if rounds > 1:
            @pl.when(both)
            def _():
                for r in range(2):
                    left_ref[:, r * size : (r + 1) * size] = left(r)
                mats = jnp.concatenate([cn_ref[modes[0]], cn_ref[modes[1]]], 1)
                total_ref[...] = dot_t(left_ref[...], mats)

        @pl.when(jnp.logical_not(both))
        def _():
            total_ref[...] = jnp.zeros_like(total_ref)

        for r in range(rounds):
            alone = ahead & present[r]

            @pl.when(alone & jnp.logical_not(both) if r < 2 else alone)
            def _():
                total_ref[...] += dot_t(left(r), cn_ref[modes[r]])

        out_ref[...] = total_ref[...].astype(BF16)

    (term,) = call(
        term_sum,
        [VM, VM, ANY] + [VM] * rounds,
        [block],
        LONG,
        size,
        factors,
        coupling_n,
        results[-1],
        *near,
        scratch=[wide, pltpu.VMEM((size, 2 * size), BF16)],
    )
    term_next = from_next(term)

    def own_sum(factor_ref, cm_ref, after_ref, *refs):
        got, out_ref = refs[:-1], refs[-1]
        out_ref[...] = jnp.zeros_like(out_ref)
        for r, ref in enumerate(got):
            mode, _, present = arriving(route[r])

            @pl.when(present)
            def _():
                out_ref[...] += couple(cm_ref[mode], scaled(ref, factor_ref, r).astype(BF16))

    (own,) = call(
        own_sum, [VM, VM, ANY] + [VM] * rounds, [wide], 2 * rounds, size, factors, coupling_m, term, *near
    )

    def real_first(factor_ref, got_ref, out_ref):
        out_ref[...] = scaled(got_ref, factor_ref, 0)

    (real_sum,) = call(real_first, [VM, VM], [wide], SHORT, size, factors, arrived[0])

    def imag_part(k, source):
        def kernel(own_ref, term_ref, source_ref, out_ref):
            last = lax.axis_index("slab") == slabs - 1

            @pl.when(is_kind(k) & jnp.logical_not(last))
            def _():
                out_ref[...] = (own_ref[...] + term_ref[...].astype(F32)).astype(BF16)

            @pl.when(is_kind(k) & last)
            def _():
                out_ref[...] = own_ref[...].astype(BF16)

            if k:

                @pl.when(is_kind(0))
                def _():
                    out_ref[...] = source_ref[...]

        return call(kernel, [VM, VM, VM if k else ANY], [block], SHORT, size, own, term_next[k], source)[0]

    imag_sum = imag_part(1, imag_part(0, real_sum))

    def finish(factor_ref, imag_ref, real_ref, *refs):
        got, out_ref, held_ref, sems = refs[: rounds - 1], refs[-3], refs[-2], refs[-1]
        imag_copy = pltpu.make_async_copy(imag_ref, out_ref.at[0, 0, 1], sems.at[1])
        imag_copy.start()
        total = real_ref[...]
        for r, ref in enumerate(got, 1):
            total += scaled(ref, factor_ref, r)
        held_ref[...] = total.astype(BF16)
        real_copy = pltpu.make_async_copy(held_ref, out_ref.at[0, 0, 0], sems.at[0])
        real_copy.start()
        imag_copy.wait()
        real_copy.wait()

    return pl.pallas_call(
        finish,
        out_shape=jax.ShapeDtypeStruct(green.shape, BF16),
        in_specs=[VM] * (2 + rounds),
        out_specs=ANY,
        scratch_shapes=[block, pltpu.SemaphoreType.DMA((2,))],
        compiler_params=pltpu.CompilerParams(vmem_limit_bytes=24 << 20),
    )(factors, imag_sum, real_sum, *arrived[1:])


def solution(mesh):
    count, slabs = mesh.shape["energy"], mesh.shape["slab"]
    placed = (P("energy", "slab", None, None, None), P("energy", None, None), P(), P())
    return jax.shard_map(
        functools.partial(body, count, slabs, matchings(count)),
        mesh=mesh,
        in_specs=placed,
        out_specs=P("energy", "slab", None, None, None),
        check_vma=False,
    )
```
